256 devices in a mesh: dom: 16 (over x, y), col: 8 (over z), rep: 2 (over core).
Axes of the slice: x: 4, y: 4, z: 8, core: 2. Of those that a mesh axis runs over, the one named last changes fastest.
Arguments:
- density: float32 [48, 16, 10, 128, 128], P('dom', 'col', 'rep'), may hold values from -2.5 to 2.5
- pattern: int32 [48, 16, 10], P('dom', 'col', 'rep'), may hold values from -1 to 767, as said below
- filt: int32 [48, 16, 10], P('dom', 'col', 'rep'), may hold values from -1 to 767, as said below
Outputs:
- purified: float32 [48, 16, 10, 128, 128], P('dom', 'col', 'rep')
The draws below stay inside these ranges and needn't reach their ends.
Inputs may be any that keep to these rules, and one draw needn't show every extreme that they name: `pattern`: in every block row the valid entries come first and are distinct; slot 0 is the row's own cell; every valid entry names a cell at most 2 cells away along the first grid dimension and at most 1 along the second, both periodic; empty slots hold -1; some bands of rows use all 10 slots. `filt`: in every block row the valid entries come first and are distinct; slot 0 is the row's own cell; every valid entry names a cell at most 2 cells away along the first grid dimension and at most 1 along the second, both periodic; empty slots hold -1; some bands of rows use all 10 slots.
All inputs are finite; a program needn't handle non-finite values.
Results may differ from the reference program's by a relative error of at most 0.0003.
Values sent between devices are 32-bit elements; how exact they have to be, the bound alone decides.
No kernel may reach another device: no remote copies, remote signals or barrier semaphores. Data moves between devices by JAX's collectives and lax.ppermute only.
A program may use at most 128 MiB of HBM per device.

```python
import jax
import jax.numpy as jnp
from jax import lax

BS = 128
K = 10
KF = 10
GD = 48
GC = 16


def pattern_draw(key, slots):
    key_perm, key_level, key_count = jax.random.split(key, 3)
    total = GD * GC
    others = jnp.arange(14, dtype=jnp.int32)
    others = others + (others >= 7).astype(jnp.int32)
    scores = jax.random.randint(key_perm, (total, 14), 0, 1 << 20) * 16 + jnp.arange(14, dtype=jnp.int32)[None, :]
    order = jnp.argsort(scores, axis=1, stable=True)
    chosen = others[order][:, :slots - 1]
    picks = jnp.concatenate([jnp.full((total, 1), 7, jnp.int32), chosen], axis=1)
    shift_d = picks // 3 - 2
    shift_c = picks % 3 - 1
    band = jax.random.randint(key_level, (GD,), 0, 2).at[0].set(1)
    row_ids = jnp.arange(total, dtype=jnp.int32)
    cell_d = row_ids // GC
    cell_c = row_ids % GC
    row_band = band[cell_d]
    loose = jax.random.randint(key_count, (total,), 3, slots - 1)
    counts = jnp.where(row_band == 1, slots, jnp.minimum(loose, slots))
    target = (cell_d[:, None] + shift_d) % GD * GC + (cell_c[:, None] + shift_c) % GC
    valid = jnp.arange(slots, dtype=jnp.int32)[None, :] < counts[:, None]
    return jnp.where(valid, target, -1).astype(jnp.int32).reshape(GD, GC, slots)


def draw_pattern(key, part):
    key = jax.random.fold_in(key, 11)
    return pattern_draw(key, K)


def draw_filt(key, part):
    key = jax.random.fold_in(key, 23)
    return pattern_draw(key, KF)


def shard_levels(key, shape, shards, least, high):
    level = 1.0
    for dim, parts in shards:
        draws = jax.random.uniform(jax.random.fold_in(jax.random.fold_in(key, 6), dim), (parts,), jnp.float32, least / len(shards), high / len(shards))
        level = level * jnp.repeat(jnp.exp(draws), shape[dim] // parts).reshape((-1,) + (1,) * (len(shape) - 1 - dim))
    return level


def centred(key, dims, scale, most, cuts=(), kind=jnp.bfloat16):
    result = jax.random.normal(key, dims, jnp.float32) * scale
    if len(cuts) > 0:
        result = shard_levels(key, dims, cuts, -0.22, 0.18) * result
    return jnp.clip(result, min=-most, max=most).astype(kind)


def setup_inputs(seed: int = 0) -> dict:
    keys = jax.random.split(jax.random.key(seed), 4)
    return {
        "density": centred(keys[0], (GD, GC, K, BS, BS), ((K * BS) ** -0.25), 2.5, ((0, 16), (1, 8), (2, 2)), jnp.float32),
        "pattern": draw_pattern(jax.random.fold_in(keys[3], 71), 0),
        "filt": draw_filt(jax.random.fold_in(keys[3], 71), 0),
    }


def matched(block_cols, left_cols, want_cols):
    table = (block_cols[:, None, :] == want_cols[None, :, None])
    table = table & (left_cols[:, None, None] >= 0) & (want_cols[None, :, None] >= 0)
    return table


def reference(density, pattern, filt):
    grid_d = density.shape[0]
    grid_c = density.shape[1]
    total = grid_d * grid_c
    width = density.shape[3]
    values = density.reshape(total, density.shape[2], width, width)
    columns = pattern.reshape(total, pattern.shape[2])
    targets = filt.reshape(total, filt.shape[2])

    def product(left_all, cols_all):
        def one_row(row_item):
            left_vals, left_cols, want_cols = row_item
            where_rows = jnp.clip(left_cols, 0, total - 1).astype(jnp.int32)
            block_rows = values[where_rows]
            block_cols = columns[where_rows]
            table = matched(block_cols, left_cols, want_cols).astype(values.dtype)
            picked = jnp.einsum("sft,stab->sfab", table, block_rows, precision=lax.Precision.HIGHEST)
            return jnp.einsum("sab,sfbc->fac", left_vals, picked, precision=lax.Precision.HIGHEST)
        return lax.map(one_row, (left_all, cols_all, targets))

    square = product(values, columns)
    cube = product(square, targets)
    purified = 3.0 * square - 2.0 * cube
    return purified.reshape(grid_d, grid_c, targets.shape[1], width, width)
```

```python
import functools

import jax
import jax.numpy as jnp
import numpy as np
from jax import lax
from jax.experimental import pallas as pl
from jax.experimental.pallas import tpu as pltpu
from jax.sharding import PartitionSpec as P

UNROLL = 16
ROWS, COLS = 3, 2
HALF = 5
CUTS = ((2, 3), (3, 2))
RIM_D, RIM_C = ROWS + 4, COLS + 2
RIM = RIM_D * RIM_C
CELLS = ROWS * COLS
SLOTS = 2 * HALF
OWN = 60
EARLY = 200
LATE = 40
ZERO = EARLY + 2 * LATE
TOTAL = ZERO + 1
SPOT = OWN


def block_places():
    places = np.zeros((2, RIM, HALF), np.int32)
    by_col, by_dom = corner_slots()
    for other in range(2):
        for rd in range(RIM_D):
            for rc in range(RIM_C):
                for s in range(HALF):
                    mid_d, mid_c = 2 <= rd < 2 + ROWS, 1 <= rc < 1 + COLS
                    low, far = int(rd >= 2 + ROWS), int(rc == RIM_C - 1)
                    row = rd - 2 - ROWS if low else rd
                    if mid_d and mid_c:
                        at = other * 30 + ((rd - 2) * 2 + rc - 1) * 5 + s
                    elif mid_d:
                        at = 60 + other * 30 + far * 15 + (rd - 2) * 5 + s
                    elif mid_c:
                        at = 120 + other * 40 + low * 20 + (row * 2 + rc - 1) * 5 + s
                    elif (low, row, s) in by_col:
                        at = EARLY + other * LATE + far * 10 + by_col.index((low, row, s))
                    else:
                        at = EARLY + other * LATE + 20 + low * 10 + by_dom[low].index((far, row, s))
                    places[other, rd * RIM_C + rc, s] = at
    return places


def corner_slots():
    by_col = [(low, row, s) for low in range(2) for row in range(2) for s in range(CUTS[low][row])]
    by_dom = [
        [(far, row, s) for far in range(2) for row in range(2) for s in range(CUTS[low][row], HALF)] for low in range(2)
    ]
    return by_col, by_dom


def shift(array, axis, step):
    peers = lax.axis_size(axis)
    return lax.ppermute(array, axis, [(i, (i + step) % peers) for i in range(peers)])


SQUARE_LEN = SPOT * SLOTS + 2 * UNROLL
CUBE_LEN = CELLS * HALF * SLOTS + 2 * UNROLL
TAIL_LEN = 2 * CELLS * HALF * SLOTS + 2 * UNROLL
LANES = 128
NONE = RIM + 3
TABLE = 32


def list_kernel(
    grid, known, stored, first, early, late, late_other, cube, tail, touched, counts, table_v, place_v, table, place, flag, sems
):
    grid_d, grid_c = grid
    dom, col, rep = lax.axis_index("dom"), lax.axis_index("col"), lax.axis_index("rep")
    lane = lax.broadcasted_iota(jnp.int32, (1, LANES), 1)
    names = jnp.full((1, LANES), -5, jnp.int32)
    name = []
    for j in range(RIM):
        d, c = dom * ROWS + (j // RIM_C - 2), col * COLS + (j % RIM_C - 1)
        d = jnp.where(d < 0, d + grid_d, jnp.where(d >= grid_d, d - grid_d, d))
        c = jnp.where(c < 0, c + grid_c, jnp.where(c >= grid_c, c - grid_c, c))
        name.append(d * grid_c + c)
        names = jnp.where(lane == j, name[j], names)
    table_v[...] = jnp.full((TABLE, LANES), -1, jnp.int32)
    for r in range(RIM_D):
        x, at = known[r], stored[r]
        row = jnp.full((RIM_C, LANES), -1, jnp.int32)
        for t in range(SLOTS):
            row = jnp.where(x[:, t:t + 1] == names, at[:, t:t + 1], row)
        table_v[r * RIM_C:(r + 1) * RIM_C, :] = row
    one = pltpu.make_async_copy(table_v, table, sems.at[0])
    one.start()
    for q in range(2):
        for r in range(ROWS):
            x = known[2 + r, 1:1 + COLS] if q == 0 else known[RIM_D + r, :COLS]
            at = jnp.full((COLS, SLOTS), NONE, jnp.int32)
            for j in range(RIM):
                at = jnp.where(x == name[j], j, at)
            place_v[q * CELLS + r * COLS:q * CELLS + (r + 1) * COLS, :SLOTS] = at
    two = pltpu.make_async_copy(place_v, place, sems.at[1])
    two.start()
    two.wait()
    one.wait()

    blank = ZERO | (ZERO << 10) | (SPOT << 20)
    blank_cube = 2 * SPOT | (ZERO << 10) | ((CELLS * HALF) << 20)

    def pad(ref, n, code):
        ref[n] = code
        return n + (n & 1)

    def square_cell(i, carry):
        rows = [place[i, s] for s in range(SLOTS)]
        own = [i * HALF + s % HALF + jnp.where(rep == s // HALF, 0, CELLS * HALF) for s in range(SLOTS)]

        def square_row(f, carry):
            nf, ne, nl, no, nt = carry
            before = nl + no
            k = place[CELLS + i, f]
            spot = i * SLOTS + f
            o = spot << 20
            values = [table[j, k] for j in rows]
            for s in range(SLOTS):
                v = values[s]
                code = own[s] | (v << 10) | o
                first[nf] = code
                early[ne] = code
                late[nl] = code
                late_other[no] = code
                third, second = jnp.where(v >= EARLY + LATE, 1, 0), jnp.where(v >= EARLY, 1, 0)
                beyond = jnp.where(v >= OWN, 1, 0)
                nf = nf + jnp.where(v >= 0, 1, 0) - beyond
                ne = ne + beyond - second
                nl = nl + second - third
                no = no + third
            again = jnp.where(nl + no > before, 1, 0)
            flag[spot] = again
            touched[nt] = spot
            nf, ne = pad(first, nf, blank), pad(early, ne, blank)
            return nf, ne, pad(late, nl, blank), pad(late_other, no, blank), nt + again

        return lax.fori_loop(0, SLOTS, square_row, carry)

    def cube_cell(i, carry):
        rows = [place[CELLS + i, g] for g in range(SLOTS)]
        again = [flag[i * SLOTS + g] for g in range(SLOTS)]

        def cube_row(f, carry):
            nc, nt = carry
            k = place[CELLS + i, rep * HALF + f]
            o = (i * SLOTS) | ((i * HALF + f) << 20)
            values = [table[j, k] for j in rows]
            for g in range(SLOTS):
                v = values[g]
                code = (o + (g + SPOT)) | (v << 10)
                hit, is_late = jnp.where(v >= 0, 1, 0), jnp.where(v >= EARLY, 1, 0)
                cube[nc] = code
                nc = nc + hit - is_late
                tail[nt] = code
                nt = nt + is_late
                tail[nt] = code - SPOT
                nt = nt + hit * again[g]
            return pad(cube, nc, blank_cube), pad(tail, nt, blank_cube)

        return lax.fori_loop(0, HALF, cube_row, carry)

    zero = jnp.int32(0)
    nf, ne, nl, no, touches = lax.fori_loop(0, CELLS, square_cell, (zero,) * 5)
    nc, nt = lax.fori_loop(0, CELLS, cube_cell, (zero, zero))
    for u in range(2 * UNROLL):
        first[nf + u] = blank
        early[ne + u] = blank
        late[nl + u] = blank
        late_other[no + u] = blank
        cube[nc + u] = blank_cube
        tail[nt + u] = blank_cube
    for q, n in enumerate((nf, ne, nl, no, nc, nt)):
        counts[q] = n // 2
    counts[6] = touches
    counts[7] = rep * HALF


def make_lists(known, stored):
    grid = (ROWS * lax.axis_size("dom"), COLS * lax.axis_size("col"))
    lengths = (SQUARE_LEN,) * 4 + (CUBE_LEN, TAIL_LEN, SPOT + 1, 8)
    return pl.pallas_call(
        functools.partial(list_kernel, grid),
        out_shape=[jax.ShapeDtypeStruct((n,), jnp.int32) for n in lengths],
        in_specs=[vmem()] * 2,
        out_specs=[smem()] * len(lengths),
        scratch_shapes=[
            pltpu.VMEM((TABLE, LANES), jnp.int32),
            pltpu.VMEM((16, LANES), jnp.int32),
            pltpu.SMEM((TABLE, LANES), jnp.int32),
            pltpu.SMEM((16, LANES), jnp.int32),
            pltpu.SMEM((SPOT,), jnp.int32),
            pltpu.SemaphoreType.DMA((2,)),
        ],
        compiler_params=pltpu.CompilerParams(vmem_limit_bytes=2 << 20),
        cost_estimate=pl.CostEstimate(flops=1000, bytes_accessed=1000, transcendentals=0),
        name="lists",
    )(known, stored)


def split(x):
    high = x.astype(jnp.bfloat16)
    low = (x - high.astype(jnp.float32)).astype(jnp.bfloat16)
    return high, low


def split_blocks(src, src_at, dst, dst_at, count):
    def step(b, _):
        high, low = split(src[src_at + b])
        dst[dst_at + b, :, :128] = high
        dst[dst_at + b, :, 128:] = low
        return 0

    lax.fori_loop(0, count, step, 0, unroll=2)


def run_list(codes, pairs, left, right, total, unroll=UNROLL):
    def step(at, _):
        for u in range(unroll):
            first = codes[at * (2 * unroll) + 2 * u]
            second = codes[at * (2 * unroll) + 2 * u + 1]
            l1, r1 = first & 1023, (first >> 10) & 1023
            l2, r2 = second & 1023, (second >> 10) & 1023
            o = first >> 20
            a1, a2 = left[l1], left[l2]
            lhs = jnp.concatenate(
                [
                    jnp.concatenate([a1[:, :128], a2[:, :128]], axis=1),
                    jnp.concatenate([a1[:, 128:], a2[:, 128:]], axis=1),
                ],
                axis=0,
            )
            rhs = jnp.concatenate([right[r1], right[r2]], axis=0)
            out = jnp.dot(lhs, rhs, preferred_element_type=jnp.float32)
            total[o] += (out[:128, :128] + out[:128, 128:]) + (out[128:, :128] + out[128:, 128:])
        return 0

    lax.fori_loop(0, (pairs + unroll - 1) // unroll, step, 0)


def zero_blocks(ref, count):
    def step(b, _):
        ref[b] = jnp.zeros(ref.shape[1:], ref.dtype)
        return 0

    lax.fori_loop(0, count, step, 0)


DEPTH, CHUNK = 3, 20


def chunks(pieces):
    result, at = [], 0
    for piece in pieces:
        parts = -(-piece.shape[0] // CHUNK)
        size = piece.shape[0] // parts
        for part in range(parts):
            result.append((piece, part * size, size, at))
            at += size
    return result


def load_and_split(pieces, stage, sems, blocks, base, prepare=lambda: None):
    copies, parts = [], chunks(pieces)
    for n, (piece, start, size, _) in enumerate(parts):
        slot = stage.at[pl.ds(n % DEPTH * CHUNK, size)]
        copies.append(pltpu.make_async_copy(piece.at[pl.ds(start, size)], slot, sems.at[n]))
    for copy in copies[:DEPTH]:
        copy.start()
    prepare()
    for n, (_, _, size, at) in enumerate(parts):
        copies[n].wait()
        split_blocks(stage, n % DEPTH * CHUNK, blocks, base + at, size)
        if n + DEPTH < len(parts):
            copies[n + DEPTH].start()


def first_kernel(codes, counts, *refs):
    pieces, (blocks, square, stage, sems) = refs[:-4], refs[-4:]

    def prepare():
        blocks[ZERO] = jnp.zeros(blocks.shape[1:], blocks.dtype)
        zero_blocks(square, SPOT + 1)

    load_and_split(pieces, stage, sems, blocks, 0, prepare)
    run_list(codes, counts[0], blocks, blocks, square)


def early_kernel(codes, cube_codes, counts, _, square_in, *refs):
    pieces, (blocks, square, halves, cube, stage, sems) = refs[:-6], refs[-6:]

    def prepare():
        zero_blocks(cube, CELLS * HALF + 1)
        halves[2 * SPOT] = jnp.zeros(blocks.shape[1:], blocks.dtype)

    load_and_split(pieces, stage, sems, blocks, OWN, prepare)
    run_list(codes, counts[1], blocks, blocks, square)
    split_blocks(square, 0, halves, SPOT, SPOT)
    run_list(cube_codes, counts[4], halves, blocks, cube)
    base = counts[7]

    def combine(i, _):
        for f in range(HALF):
            cube[i * HALF + f] = cube[i * HALF + f] - 1.5 * square[i * SLOTS + base + f]
        return 0

    lax.fori_loop(0, CELLS, combine, 0)
    zero_blocks(square, SPOT + 1)


def corner_kernel(codes, counts, blocks_in, square_in, *refs):
    pieces, (blocks, square, stage, sems) = refs[:-4], refs[-4:]
    load_and_split(pieces, stage, sems, blocks, EARLY)
    run_list(codes, counts[2], blocks, blocks, square, 8)


def late_kernel(codes, tail_codes, touched, counts, blocks_in, square_in, halves_in, cube_in, *refs):
    pieces, (out, blocks, square, halves, cube, stage, sems) = refs[:-7], refs[-7:]
    load_and_split(pieces, stage, sems, blocks, EARLY + LATE)
    run_list(codes, counts[3], blocks, blocks, square, 8)

    def resplit(n, _):
        o = touched[n]
        high, low = split(square[o])
        halves[o, :, :128] = high
        halves[o, :, 128:] = low
        return 0

    lax.fori_loop(0, counts[6], resplit, 0)
    run_list(tail_codes, counts[5], halves, blocks, cube, 8)
    base = counts[7]
    copies = []
    for i in range(CELLS):
        for f in range(HALF):
            o = i * HALF + f
            stage[o] = 3.0 * square[i * SLOTS + base + f] - 2.0 * cube[o]
        at = pl.ds(i * HALF, HALF)
        copies.append(pltpu.make_async_copy(stage.at[at], out.at[at], sems.at[i]))
        copies[-1].start()
    for copy in copies:
        copy.wait()


def pack_kernel(plan, count, *refs):
    sources, dests, sems = refs[:count], refs[count:-1], refs[-1]
    copies = []
    for n, (d, at, q, start, length) in enumerate(plan):
        copies.append(pltpu.make_async_copy(sources[q].at[pl.ds(start, length)], dests[d].at[pl.ds(at, length)], sems.at[n]))
        copies[-1].start()
    for copy in copies:
        copy.wait()


def pack(arrays, wanted):
    plan, sizes = [], []
    for d, ranges in enumerate(wanted):
        at = 0
        for q, start, length in ranges:
            plan.append((d, at, q, start, length))
            at += length
        sizes.append(at)
    return pl.pallas_call(
        functools.partial(pack_kernel, tuple(plan), len(arrays)),
        out_shape=[jax.ShapeDtypeStruct((n, 128, 128), jnp.float32) for n in sizes],
        in_specs=[anyspace()] * len(arrays),
        out_specs=[vmem()] * len(sizes),
        scratch_shapes=[pltpu.SemaphoreType.DMA((len(plan),))],
        compiler_params=pltpu.CompilerParams(vmem_limit_bytes=6 << 20),
        cost_estimate=pl.CostEstimate(flops=1000, bytes_accessed=1000, transcendentals=0),
        name="pack",
    )(*arrays)


def smem():
    return pl.BlockSpec(memory_space=pltpu.SMEM)


def anyspace():
    return pl.BlockSpec(memory_space=pl.ANY)


def vmem():
    return pl.BlockSpec(memory_space=pltpu.VMEM)


def hbm():
    return pl.BlockSpec(memory_space=pltpu.HBM)


BLOCKS = pltpu.VMEM((TOTAL, 128, 256), jnp.bfloat16)
SQUARE = pltpu.VMEM((SPOT + 1, 128, 128), jnp.float32)
HALVES = pltpu.VMEM((2 * SPOT + 1, 128, 256), jnp.bfloat16)
CUBE = pltpu.VMEM((CELLS * HALF + 1, 128, 128), jnp.float32)


def call(kernel, name, lists, held, pieces, outs, aliases):
    kinds = [hbm() if isinstance(o, jax.ShapeDtypeStruct) else vmem() for o in outs]
    return pl.pallas_call(
        kernel,
        out_shape=outs,
        in_specs=[smem()] * len(lists) + [vmem()] * len(held) + [anyspace()] * len(pieces),
        out_specs=kinds,
        scratch_shapes=[pltpu.VMEM((DEPTH * CHUNK, 128, 128), jnp.float32), pltpu.SemaphoreType.DMA((8,))],
        input_output_aliases={len(lists) + i: o for i, o in aliases.items()},
        compiler_params=pltpu.CompilerParams(vmem_limit_bytes=4 << 20),
        cost_estimate=pl.CostEstimate(flops=1000, bytes_accessed=1000, transcendentals=0),
        name=name,
    )(*lists, *held, *pieces)


def stored_places():
    mine, other = block_places()
    first = np.concatenate([mine, other], axis=1).reshape(RIM_D, RIM_C, SLOTS)
    second = np.concatenate([other, mine], axis=1).reshape(RIM_D, RIM_C, SLOTS)
    return jnp.where(lax.axis_index("rep") == 0, first, second)


def flat(x):
    return x.reshape(-1, 128, 128)


def body(density, pattern, filt):
    blocks = flat(density)
    row = COLS * HALF
    above, below = shift(pattern[1:], "dom", 1), shift(pattern[:2], "dom", -1)
    edges = [[(0, r * row + q, HALF) for r in range(ROWS)] for q in (HALF, 0)]
    edge_d, edge_u, edge_r, edge_l = pack([blocks], [[(0, row, 2 * row)], [(0, 0, 2 * row)]] + edges)
    down, up = shift(edge_d, "dom", 1), shift(edge_u, "dom", -1)
    own_other = shift(blocks, "rep", 1)
    near = jnp.concatenate([above, pattern, below], axis=0)
    before, after = shift(near[:, 1:], "col", 1), shift(near[:, :1], "col", -1)
    before, after, edge_r, edge_l = lax.optimization_barrier((before, after, edge_r, edge_l))
    right, left = shift(edge_r, "col", 1), shift(edge_l, "col", -1)
    rim = jnp.concatenate([before, near, after], axis=1)
    own_filt = jnp.pad(filt, ((0, 0), (0, RIM_C - COLS), (0, 0)), constant_values=-1)
    known = lax.all_gather(jnp.concatenate([rim, own_filt], axis=0), "rep", axis=2, tiled=True)
    first_codes, early_codes, late_codes, other_codes, cube_codes, tail_codes, touched, counts = make_lists(
        known, stored_places()
    )
    held, square = call(first_kernel, "first", [first_codes, counts], [], [blocks, own_other], [BLOCKS, SQUARE], {})
    held, square, right, left, down, up = lax.optimization_barrier((held, square, right, left, down, up))
    by_col, by_dom = corner_slots()
    to_r, to_l = [[(low, row * 10 + c * 5 + s, 1) for low, row, s in by_col] for c in (1, 0)]
    to_d, to_u = [[(2 + far, (row + 1 - low) * 5 + s, 1) for far, row, s in by_dom[low]] for low in (0, 1)]
    to_r, to_l, to_d, to_u = pack([down, up, right, left], [to_r, to_l, to_d, to_u])
    corner_r, corner_l = shift(to_r, "col", 1), shift(to_l, "col", -1)
    corner_d, corner_u = shift(to_d, "dom", 1), shift(to_u, "dom", -1)

    def with_other(*pieces):
        return list(pieces) + [shift(p, "rep", 1) for p in pieces]

    early = with_other(right, left) + with_other(down, up)
    held, square, halves, cube = call(
        early_kernel, "early", [early_codes, cube_codes, counts], [held, square], early,
        [BLOCKS, SQUARE, HALVES, CUBE], {0: 0, 1: 1},
    )
    held, square, halves, cube, *corners = lax.optimization_barrier(
        (held, square, halves, cube, corner_r, corner_l, corner_d, corner_u)
    )
    others = [shift(p, "rep", 1) for p in corners]
    held, square = call(
        corner_kernel, "corner", [late_codes, counts], [held, square], corners, [BLOCKS, SQUARE], {0: 0, 1: 1}
    )
    out = jax.ShapeDtypeStruct((CELLS * HALF, 128, 128), jnp.float32)
    out = call(
        late_kernel, "late", [other_codes, tail_codes, touched, counts], [held, square, halves, cube], others,
        [out, BLOCKS, SQUARE, HALVES, CUBE], {0: 1, 1: 2, 2: 3, 3: 4},
    )[0]
    return out.reshape(density.shape)


def solution(mesh):
    in_specs = (P("dom", "col", "rep", None, None), P("dom", "col", "rep"), P("dom", "col", "rep"))
    out_specs = P("dom", "col", "rep", None, None)
    return jax.shard_map(body, mesh=mesh, in_specs=in_specs, out_specs=out_specs, check_vma=False)
```

```python
import functools

import jax
import jax.numpy as jnp
import numpy as np
from jax import lax
from jax.experimental import pallas as pl
from jax.experimental.pallas import tpu as pltpu
from jax.sharding import PartitionSpec as P

UNROLL = 32
ROWS, COLS = 3, 2
HALF = 5
RIM_D, RIM_C = ROWS + 4, COLS + 2
RIM = RIM_D * RIM_C
CELLS = ROWS * COLS
SLOTS = 2 * HALF
OWN = 60
EARLY = 200
ROWS_PART = 70
LATE = 40
ZERO = EARLY + 2 * LATE
TOTAL = ZERO + 1
SPOT = OWN


def block_places(core):
    places = np.zeros((RIM_D, RIM_C, SLOTS), np.int32)
    for rd in range(RIM_D):
        for rc in range(RIM_C):
            for t in range(SLOTS):
                half, s = divmod(t, HALF)
                other = int(half != core)
                mid_d, mid_c = 2 <= rd < 2 + ROWS, 1 <= rc < 1 + COLS
                low, far = int(rd >= 2 + ROWS), int(rc == RIM_C - 1)
                row = rd - 2 - ROWS if low else rd
                if mid_d and mid_c:
                    at = other * 30 + ((rd - 2) * 2 + rc - 1) * 5 + s
                elif mid_d:
                    at = OWN + other * ROWS_PART + far * 15 + (rd - 2) * 5 + s
                elif mid_c:
                    at = OWN + other * ROWS_PART + 30 + int(low != half) * 20 + (row * 2 + rc - 1) * 5 + s
                else:
                    at = EARLY + other * LATE + int(low != half) * 20 + far * 10 + row * 5 + s
                places[rd, rc, t] = at
    return places


def shift(array, axis, step):
    peers = lax.axis_size(axis)
    return lax.ppermute(array, axis, [(i, (i + step) % peers) for i in range(peers)])


def cross(array, step):
    peers = lax.axis_size("dom")
    pairs = [(2 * i + core, (i + (step, -step)[core]) % peers * 2 + core) for i in range(peers) for core in range(2)]
    return lax.ppermute(array, ("dom", "rep"), pairs)


SQUARE_LEN = SPOT * SLOTS + UNROLL
CUBE_LEN = CELLS * HALF * SLOTS + UNROLL
TAIL_LEN = 2 * CELLS * HALF * SLOTS + UNROLL
LANES = 128
NONE = RIM + 3
TABLE = 32


def list_kernel(
    grid, known, stored, early, late, cube, tail, touched, counts, table_v, place_v, table, place, flag, sems
):
    grid_d, grid_c = grid
    dom, col, rep = lax.axis_index("dom"), lax.axis_index("col"), lax.axis_index("rep")
    lane = lax.broadcasted_iota(jnp.int32, (1, LANES), 1)
    names = jnp.full((1, LANES), -5, jnp.int32)
    name = []
    for j in range(RIM):
        d, c = dom * ROWS + (j // RIM_C - 2), col * COLS + (j % RIM_C - 1)
        d = jnp.where(d < 0, d + grid_d, jnp.where(d >= grid_d, d - grid_d, d))
        c = jnp.where(c < 0, c + grid_c, jnp.where(c >= grid_c, c - grid_c, c))
        name.append(d * grid_c + c)
        names = jnp.where(lane == j, name[j], names)
    table_v[...] = jnp.full((TABLE, LANES), -1, jnp.int32)
    for r in range(RIM_D):
        x, at = known[r], stored[r]
        row = jnp.full((RIM_C, LANES), -1, jnp.int32)
        for t in range(SLOTS):
            row = jnp.where(x[:, t:t + 1] == names, at[:, t:t + 1], row)
        table_v[r * RIM_C:(r + 1) * RIM_C, :] = row
    one = pltpu.make_async_copy(table_v, table, sems.at[0])
    one.start()
    for q in range(2):
        for r in range(ROWS):
            x = known[2 + r, 1:1 + COLS] if q == 0 else known[RIM_D + r, :COLS]
            at = jnp.full((COLS, SLOTS), NONE, jnp.int32)
            for j in range(RIM):
                at = jnp.where(x == name[j], j, at)
            place_v[q * CELLS + r * COLS:q * CELLS + (r + 1) * COLS, :SLOTS] = at
    two = pltpu.make_async_copy(place_v, place, sems.at[1])
    two.start()
    two.wait()
    one.wait()

    blank = ZERO | (ZERO << 10) | (SPOT << 20)
    blank_cube = 2 * SPOT | (ZERO << 10) | ((CELLS * HALF) << 20)

    def square_cell(i, carry):
        rows = [place[i, s] for s in range(SLOTS)]
        own = [i * HALF + s % HALF + jnp.where(rep == s // HALF, 0, CELLS * HALF) for s in range(SLOTS)]

        def square_row(f, carry):
            ne, nl, nt = carry
            before = nl
            k = place[CELLS + i, f]
            spot = i * SLOTS + f
            o = spot << 20
            values = [table[j, k] for j in rows]
            for s in range(SLOTS):
                v = values[s]
                code = (own[s] | o) + (v << 10)
                early[ne] = code
                late[nl] = code
                is_late = jnp.where(v >= EARLY, 1, 0)
                ne = ne + jnp.where(v >= 0, 1, 0) - is_late
                nl = nl + is_late
            again = jnp.where(nl > before, 1, 0)
            flag[spot] = again
            touched[nt] = spot
            return ne, nl, nt + again

        return lax.fori_loop(0, SLOTS, square_row, carry)

    def cube_cell(i, carry):
        rows = [place[CELLS + i, g] for g in range(SLOTS)]
        again = [flag[i * SLOTS + g] for g in range(SLOTS)]

        def cube_row(f, carry):
            nc, nt = carry
            k = place[CELLS + i, rep * HALF + f]
            o = (i * SLOTS) | ((i * HALF + f) << 20)
            values = [table[j, k] for j in rows]
            for g in range(SLOTS):
                v = values[g]
                code = (o + (g + SPOT)) | (v << 10)
                hit, is_late = jnp.where(v >= 0, 1, 0), jnp.where(v >= EARLY, 1, 0)
                cube[nc] = code
                nc = nc + hit - is_late
                tail[nt] = code
                nt = nt + is_late
                tail[nt] = code - SPOT
                nt = nt + hit * again[g]
            return nc, nt

        return lax.fori_loop(0, HALF, cube_row, carry)

    zero = jnp.int32(0)
    ne, nl, touches = lax.fori_loop(0, CELLS, square_cell, (zero,) * 3)
    nc, nt = lax.fori_loop(0, CELLS, cube_cell, (zero, zero))
    for u in range(UNROLL):
        early[ne + u] = blank
        late[nl + u] = blank
        cube[nc + u] = blank_cube
        tail[nt + u] = blank_cube
    for q, n in enumerate((ne, nl, nc, nt)):
        counts[q] = n
    counts[6] = touches
    counts[7] = rep * HALF


def make_lists(known, stored):
    grid = (ROWS * lax.axis_size("dom"), COLS * lax.axis_size("col"))
    lengths = (SQUARE_LEN,) * 2 + (CUBE_LEN, TAIL_LEN, SPOT + 1, 8)
    return pl.pallas_call(
        functools.partial(list_kernel, grid),
        out_shape=[jax.ShapeDtypeStruct((n,), jnp.int32) for n in lengths],
        in_specs=[vmem()] * 2,
        out_specs=[smem()] * len(lengths),
        scratch_shapes=[
            pltpu.VMEM((TABLE, LANES), jnp.int32),
            pltpu.VMEM((16, LANES), jnp.int32),
            pltpu.SMEM((TABLE, LANES), jnp.int32),
            pltpu.SMEM((16, LANES), jnp.int32),
            pltpu.SMEM((SPOT,), jnp.int32),
            pltpu.SemaphoreType.DMA((2,)),
        ],
        compiler_params=pltpu.CompilerParams(vmem_limit_bytes=2 << 20),
        cost_estimate=pl.CostEstimate(flops=1000, bytes_accessed=1000, transcendentals=0),
        name="lists",
    )(known, stored)


def split(x):
    high = x.astype(jnp.bfloat16)
    low = (x - high.astype(jnp.float32)).astype(jnp.bfloat16)
    return high, low


def split_blocks(src, src_at, dst, dst_at, count):
    def step(b, _):
        high, low = split(src[src_at + b])
        dst[dst_at + b, :, :128] = high
        dst[dst_at + b, :, 128:] = low
        return 0

    lax.fori_loop(0, count, step, 0, unroll=2)


def run_list(codes, count, left, right, total, unroll=UNROLL):
    def step(at, _):
        for u in range(unroll):
            code = codes[at * unroll + u]
            b = right[(code >> 10) & 1023]
            out = jnp.dot(left[code & 1023], jnp.concatenate([b, b], axis=0), preferred_element_type=jnp.float32)
            total[code >> 20] += out[:, :128] + out[:, 128:]
        return 0

    lax.fori_loop(0, (count + unroll - 1) // unroll, step, 0)


def zero_blocks(ref, count):
    def step(b, _):
        ref[b] = jnp.zeros(ref.shape[1:], ref.dtype)
        return 0

    lax.fori_loop(0, count, step, 0)


DEPTH, CHUNK = 3, 20


def chunks(pieces):
    result, at = [], 0
    for piece in pieces:
        parts = -(-piece.shape[0] // CHUNK)
        size = piece.shape[0] // parts
        for part in range(parts):
            result.append((piece, part * size, size, at))
            at += size
    return result


def load_and_split(pieces, stage, sems, blocks, base, prepare=lambda: None):
    copies, parts = [], chunks(pieces)
    for n, (piece, start, size, _) in enumerate(parts):
        slot = stage.at[pl.ds(n % DEPTH * CHUNK, size)]
        copies.append(pltpu.make_async_copy(piece.at[pl.ds(start, size)], slot, sems.at[n]))
    for copy in copies[:DEPTH]:
        copy.start()
    prepare()
    for n, (_, _, size, at) in enumerate(parts):
        copies[n].wait()
        split_blocks(stage, n % DEPTH * CHUNK, blocks, base + at, size)
        if n + DEPTH < len(parts):
            copies[n + DEPTH].start()


def first_kernel(*refs):
    pieces, (blocks, square, stage, sems) = refs[:-4], refs[-4:]

    def prepare():
        blocks[ZERO] = jnp.zeros(blocks.shape[1:], blocks.dtype)
        zero_blocks(square, SPOT + 1)

    load_and_split(pieces, stage, sems, blocks, 0, prepare)


def rows_kernel(_, *refs):
    pieces, (blocks, stage, sems) = refs[:-3], refs[-3:]
    load_and_split(pieces, stage, sems, blocks, OWN)


def early_kernel(codes, cube_codes, counts, _, square_in, *refs):
    pieces, (blocks, square, halves, cube, stage, sems) = refs[:-6], refs[-6:]

    def prepare():
        zero_blocks(cube, CELLS * HALF + 1)
        halves[2 * SPOT] = jnp.zeros(blocks.shape[1:], blocks.dtype)

    load_and_split(pieces, stage, sems, blocks, OWN + ROWS_PART, prepare)
    run_list(codes, counts[0], blocks, blocks, square)
    split_blocks(square, 0, halves, SPOT, SPOT)
    run_list(cube_codes, counts[2], halves, blocks, cube)
    base = counts[7]

    def combine(i, _):
        for f in range(HALF):
            cube[i * HALF + f] = cube[i * HALF + f] - 1.5 * square[i * SLOTS + base + f]
        return 0

    lax.fori_loop(0, CELLS, combine, 0)
    zero_blocks(square, SPOT + 1)


def corner_kernel(_, *refs):
    pieces, (blocks, stage, sems) = refs[:-3], refs[-3:]
    load_and_split(pieces, stage, sems, blocks, EARLY)


def late_kernel(codes, tail_codes, touched, counts, blocks_in, square_in, halves_in, cube_in, *refs):
    pieces, (out, blocks, square, halves, cube, stage, sems) = refs[:-7], refs[-7:]
    load_and_split(pieces, stage, sems, blocks, EARLY + LATE)
    run_list(codes, counts[1], blocks, blocks, square, 8)

    def resplit(n, _):
        o = touched[n]
        high, low = split(square[o])
        halves[o, :, :128] = high
        halves[o, :, 128:] = low
        return 0

    lax.fori_loop(0, counts[6], resplit, 0)
    run_list(tail_codes, counts[3], halves, blocks, cube, 16)
    base = counts[7]
    copies = []
    for i in range(CELLS):
        for f in range(HALF):
            o = i * HALF + f
            stage[o] = 3.0 * square[i * SLOTS + base + f] - 2.0 * cube[o]
        at = pl.ds(i * HALF, HALF)
        copies.append(pltpu.make_async_copy(stage.at[at], out.at[at], sems.at[i]))
        copies[-1].start()
    for copy in copies:
        copy.wait()


def pack_kernel(plan, count, *refs):
    sources, dests, sems = refs[:count], refs[count:-1], refs[-1]
    run_plan(plan, sources, dests, sems)


def pack_far_kernel(plan, source, *refs):
    dests, held, sems = refs[:-2], refs[-2], refs[-1]
    copy = pltpu.make_async_copy(source, held, sems.at[0])
    copy.start()
    copy.wait()
    run_plan(plan, [held], dests, sems)


def run_plan(plan, sources, dests, sems):
    copies = []
    rep = lax.axis_index("rep")
    for n, (d, at, q, start, length) in enumerate(plan):
        if isinstance(start, tuple):
            start = jnp.where(rep == 0, start[0], start[1])
        copies.append(pltpu.make_async_copy(sources[q].at[pl.ds(start, length)], dests[d].at[pl.ds(at, length)], sems.at[n]))
        copies[-1].start()
    for copy in copies:
        copy.wait()


def pack(arrays, wanted, far=False):
    plan, sizes = [], []
    for d, ranges in enumerate(wanted):
        at = 0
        for q, start, length in ranges:
            plan.append((d, at, q, start, length))
            at += length
        sizes.append(at)
    out = pltpu.HBM if far else jax.ShapeDtypeStruct
    held = [pltpu.VMEM(arrays[0].shape, jnp.float32)] if far else []
    kernel = functools.partial(pack_far_kernel, tuple(plan)) if far else functools.partial(pack_kernel, tuple(plan), len(arrays))
    return pl.pallas_call(
        kernel,
        out_shape=[out((n, 128, 128), jnp.float32) for n in sizes],
        in_specs=[anyspace()] * len(arrays),
        out_specs=[hbm() if far else vmem()] * len(sizes),
        scratch_shapes=held + [pltpu.SemaphoreType.DMA((len(plan),))],
        compiler_params=pltpu.CompilerParams(vmem_limit_bytes=3 << 20),
        cost_estimate=pl.CostEstimate(flops=1000, bytes_accessed=1000, transcendentals=0),
        name="pack",
    )(*arrays)


def smem():
    return pl.BlockSpec(memory_space=pltpu.SMEM)


def anyspace():
    return pl.BlockSpec(memory_space=pl.ANY)


def vmem():
    return pl.BlockSpec(memory_space=pltpu.VMEM)


def hbm():
    return pl.BlockSpec(memory_space=pltpu.HBM)


BLOCKS = pltpu.VMEM((TOTAL, 128, 256), jnp.bfloat16)
SQUARE = pltpu.VMEM((SPOT + 1, 128, 128), jnp.float32)
HALVES = pltpu.VMEM((2 * SPOT + 1, 128, 256), jnp.bfloat16)
CUBE = pltpu.VMEM((CELLS * HALF + 1, 128, 128), jnp.float32)


def call(kernel, name, lists, held, pieces, outs, aliases):
    kinds = [hbm() if isinstance(o, jax.ShapeDtypeStruct) else vmem() for o in outs]
    return pl.pallas_call(
        kernel,
        out_shape=outs,
        in_specs=[smem()] * len(lists) + [vmem()] * len(held) + [anyspace()] * len(pieces),
        out_specs=kinds,
        scratch_shapes=[pltpu.VMEM((DEPTH * CHUNK, 128, 128), jnp.float32), pltpu.SemaphoreType.DMA((16,))],
        input_output_aliases={len(lists) + i: o for i, o in aliases.items()},
        compiler_params=pltpu.CompilerParams(vmem_limit_bytes=4 << 20),
        cost_estimate=pl.CostEstimate(flops=1000, bytes_accessed=1000, transcendentals=0),
        name=name,
    )(*lists, *held, *pieces)


def stored_places():
    return jnp.where(lax.axis_index("rep") == 0, block_places(0), block_places(1))


def flat(x):
    return x.reshape(-1, 128, 128)


def body(density, pattern, filt):
    blocks = flat(density)
    row = COLS * HALF
    above, below = shift(pattern[1:], "dom", 1), shift(pattern[:2], "dom", -1)
    own_other = shift(blocks, "rep", 1)
    one, two = pack([blocks], [[(0, (row, 0), 2 * row)], [(0, (0, row), 2 * row)]], far=True)
    above, below, one = lax.optimization_barrier((above, below, one))
    one = cross(one, 1)
    near = jnp.concatenate([above, pattern, below], axis=0)
    before, after = shift(near[:, 1:], "col", 1), shift(near[:, :1], "col", -1)
    edge_r, edge_l = pack([blocks], [[(0, r * row + q, HALF) for r in range(ROWS)] for q in (HALF, 0)])
    before, after, two, edge_r, edge_l = lax.optimization_barrier((before, after, two, edge_r, edge_l))
    two = cross(two, -1)
    right, left = shift(edge_r, "col", 1), shift(edge_l, "col", -1)
    rim = jnp.concatenate([before, near, after], axis=1)
    own_filt = jnp.pad(filt, ((0, 0), (0, RIM_C - COLS), (0, 0)), constant_values=-1)
    known = lax.all_gather(jnp.concatenate([rim, own_filt], axis=0), "rep", axis=2, tiled=True)
    early_codes, late_codes, cube_codes, tail_codes, touched, counts = make_lists(known, stored_places())
    counts, own_other = lax.optimization_barrier((counts, own_other))
    held, square = call(first_kernel, "first", [], [], [blocks, own_other], [BLOCKS, SQUARE], {})
    held, square, one = lax.optimization_barrier((held, square, one))
    to_r, to_l = pack([one], [[(0, q, HALF), (0, row + q, HALF)] for q in (HALF, 0)])
    corner_r, corner_l = shift(to_r, "col", 1), shift(to_l, "col", -1)
    right, left, to_r, to_l = lax.optimization_barrier((right, left, to_r, to_l))
    (corner,) = pack([right, left], [[(q, (0, HALF), 2 * HALF) for q in (0, 1)]])
    right, left, two, corner = lax.optimization_barrier((right, left, two, corner))
    corner = cross(corner, -1)
    mine = [right, left, one, two]
    others = [shift(p, "rep", 1) for p in mine]
    (held,) = call(rows_kernel, "rows", [], [held], mine, [BLOCKS], {0: 0})
    held, square, halves, cube = call(
        early_kernel, "early", [early_codes, cube_codes, counts], [held, square], others,
        [BLOCKS, SQUARE, HALVES, CUBE], {0: 0, 1: 1},
    )
    held, square, halves, cube, *corners = lax.optimization_barrier(
        (held, square, halves, cube, corner_r, corner_l, corner)
    )
    others = [shift(p, "rep", 1) for p in corners]
    (held,) = call(corner_kernel, "corner", [], [held], corners, [BLOCKS], {0: 0})
    out = jax.ShapeDtypeStruct((CELLS * HALF, 128, 128), jnp.float32)
    out = call(
        late_kernel, "late", [late_codes, tail_codes, touched, counts], [held, square, halves, cube], others,
        [out, BLOCKS, SQUARE, HALVES, CUBE], {0: 1, 1: 2, 2: 3, 3: 4},
    )[0]
    return out.reshape(density.shape)


def solution(mesh):
    in_specs = (P("dom", "col", "rep", None, None), P("dom", "col", "rep"), P("dom", "col", "rep"))
    out_specs = P("dom", "col", "rep", None, None)
    return jax.shard_map(body, mesh=mesh, in_specs=in_specs, out_specs=out_specs, check_vma=False)
```

```python
import functools

import jax
import jax.numpy as jnp
import numpy as np
from jax import lax
from jax.experimental import pallas as pl
from jax.experimental.pallas import tpu as pltpu
from jax.sharding import PartitionSpec as P

UNROLL = 32
ROWS, COLS = 3, 2
HALF = 5
RIM_D, RIM_C = ROWS + 4, COLS + 2
RIM = RIM_D * RIM_C
CELLS = ROWS * COLS
SLOTS = 2 * HALF
OWN = 60
EARLY = 200
ROWS_PART = 70
LATE = 40
ZERO = EARLY + 2 * LATE
TOTAL = ZERO + 1
SPOT = OWN


def block_places(core):
    places = np.zeros((RIM_D, RIM_C, SLOTS), np.int32)
    for rd in range(RIM_D):
        for rc in range(RIM_C):
            for t in range(SLOTS):
                half, s = divmod(t, HALF)
                other = int(half != core)
                mid_d, mid_c = 2 <= rd < 2 + ROWS, 1 <= rc < 1 + COLS
                low, far = int(rd >= 2 + ROWS), int(rc == RIM_C - 1)
                row = rd - 2 - ROWS if low else rd
                if mid_d and mid_c:
                    at = other * 30 + ((rd - 2) * 2 + rc - 1) * 5 + s
                elif mid_d:
                    at = OWN + other * ROWS_PART + far * 15 + (rd - 2) * 5 + s
                elif mid_c:
                    at = OWN + other * ROWS_PART + 30 + int(low != half) * 20 + (row * 2 + rc - 1) * 5 + s
                else:
                    at = EARLY + other * LATE + int(low != half) * 20 + far * 10 + row * 5 + s
                places[rd, rc, t] = at
    return places


def shift(array, axis, step):
    peers = lax.axis_size(axis)
    return lax.ppermute(array, axis, [(i, (i + step) % peers) for i in range(peers)])


def cross(array, step):
    peers = lax.axis_size("dom")
    pairs = [(2 * i + core, (i + (step, -step)[core]) % peers * 2 + core) for i in range(peers) for core in range(2)]
    return lax.ppermute(array, ("dom", "rep"), pairs)


SQUARE_LEN = SPOT * SLOTS + UNROLL
CUBE_LEN = CELLS * HALF * SLOTS + UNROLL
TAIL_LEN = 2 * CELLS * HALF * SLOTS + UNROLL
LANES = 128
NONE = RIM + 3
TABLE = 32


def list_kernel(
    grid, known, stored, early, late, cube, tail, touched, counts, table_v, place_v, table, place, flag, sems
):
    grid_d, grid_c = grid
    dom, col, rep = lax.axis_index("dom"), lax.axis_index("col"), lax.axis_index("rep")
    lane = lax.broadcasted_iota(jnp.int32, (1, LANES), 1)
    names = jnp.full((1, LANES), -5, jnp.int32)
    name = []
    for j in range(RIM):
        d, c = dom * ROWS + (j // RIM_C - 2), col * COLS + (j % RIM_C - 1)
        d = jnp.where(d < 0, d + grid_d, jnp.where(d >= grid_d, d - grid_d, d))
        c = jnp.where(c < 0, c + grid_c, jnp.where(c >= grid_c, c - grid_c, c))
        name.append(d * grid_c + c)
        names = jnp.where(lane == j, name[j], names)
    table_v[...] = jnp.full((TABLE, LANES), -1, jnp.int32)
    for r in range(RIM_D):
        x, at = known[r], stored[r]
        row = jnp.full((RIM_C, LANES), -1, jnp.int32)
        for t in range(SLOTS):
            row = jnp.where(x[:, t:t + 1] == names, at[:, t:t + 1], row)
        table_v[r * RIM_C:(r + 1) * RIM_C, :] = row
    one = pltpu.make_async_copy(table_v, table, sems.at[0])
    one.start()
    for q in range(2):
        for r in range(ROWS):
            x = known[2 + r, 1:1 + COLS] if q == 0 else known[RIM_D + r, :COLS]
            at = jnp.full((COLS, SLOTS), NONE, jnp.int32)
            for j in range(RIM):
                at = jnp.where(x == name[j], j, at)
            place_v[q * CELLS + r * COLS:q * CELLS + (r + 1) * COLS, :SLOTS] = at
    two = pltpu.make_async_copy(place_v, place, sems.at[1])
    two.start()
    two.wait()
    one.wait()

    blank = ZERO | (ZERO << 10) | (SPOT << 20)
    blank_cube = 2 * SPOT | (ZERO << 10) | ((CELLS * HALF) << 20)

    def square_cell(i, carry):
        rows = [place[i, s] for s in range(SLOTS)]
        own = [i * HALF + s % HALF + jnp.where(rep == s // HALF, 0, CELLS * HALF) for s in range(SLOTS)]

        def square_row(f, carry):
            ne, nl, nt = carry
            before = nl
            k = place[CELLS + i, f]
            spot = i * SLOTS + f
            o = spot << 20
            values = [table[j, k] for j in rows]
            for s in range(SLOTS):
                v = values[s]
                code = (own[s] | o) + (v << 10)
                early[ne] = code
                late[nl] = code
                is_late = jnp.where(v >= EARLY, 1, 0)
                ne = ne + jnp.where(v >= 0, 1, 0) - is_late
                nl = nl + is_late
            again = jnp.where(nl > before, 1, 0)
            flag[spot] = again
            touched[nt] = spot
            return ne, nl, nt + again

        return lax.fori_loop(0, SLOTS, square_row, carry)

    def cube_cell(i, carry):
        rows = [place[CELLS + i, g] for g in range(SLOTS)]
        again = [flag[i * SLOTS + g] for g in range(SLOTS)]

        def cube_row(f, carry):
            nc, nt = carry
            k = place[CELLS + i, rep * HALF + f]
            o = (i * SLOTS) | ((i * HALF + f) << 20)
            values = [table[j, k] for j in rows]
            for g in range(SLOTS):
                v = values[g]
                code = (o + (g + SPOT)) | (v << 10)
                hit, is_late = jnp.where(v >= 0, 1, 0), jnp.where(v >= EARLY, 1, 0)
                cube[nc] = code
                nc = nc + hit - is_late
                tail[nt] = code
                nt = nt + is_late
                tail[nt] = code - SPOT
                nt = nt + hit * again[g]
            return nc, nt

        return lax.fori_loop(0, HALF, cube_row, carry)

    zero = jnp.int32(0)
    ne, nl, touches = lax.fori_loop(0, CELLS, square_cell, (zero,) * 3)
    nc, nt = lax.fori_loop(0, CELLS, cube_cell, (zero, zero))
    for u in range(UNROLL):
        early[ne + u] = blank
        late[nl + u] = blank
        cube[nc + u] = blank_cube
        tail[nt + u] = blank_cube
    for q, n in enumerate((ne, nl, nc, nt)):
        counts[q] = n
    counts[6] = touches
    counts[7] = rep * HALF


def make_lists(known, stored):
    grid = (ROWS * lax.axis_size("dom"), COLS * lax.axis_size("col"))
    lengths = (SQUARE_LEN,) * 2 + (CUBE_LEN, TAIL_LEN, SPOT + 1, 8)
    return pl.pallas_call(
        functools.partial(list_kernel, grid),
        out_shape=[jax.ShapeDtypeStruct((n,), jnp.int32) for n in lengths],
        in_specs=[vmem()] * 2,
        out_specs=[smem()] * len(lengths),
        scratch_shapes=[
            pltpu.VMEM((TABLE, LANES), jnp.int32),
            pltpu.VMEM((16, LANES), jnp.int32),
            pltpu.SMEM((TABLE, LANES), jnp.int32),
            pltpu.SMEM((16, LANES), jnp.int32),
            pltpu.SMEM((SPOT,), jnp.int32),
            pltpu.SemaphoreType.DMA((2,)),
        ],
        compiler_params=pltpu.CompilerParams(vmem_limit_bytes=2 << 20),
        cost_estimate=pl.CostEstimate(flops=1000, bytes_accessed=1000, transcendentals=0),
        name="lists",
    )(known, stored)


def split(x):
    high = x.astype(jnp.bfloat16)
    low = (x - high.astype(jnp.float32)).astype(jnp.bfloat16)
    return high, low


def split_blocks(src, src_at, dst, dst_at, count):
    def step(b, _):
        high, low = split(src[src_at + b])
        dst[dst_at + b, :, :128] = high
        dst[dst_at + b, :, 128:] = low
        return 0

    lax.fori_loop(0, count, step, 0, unroll=2)


def run_list(codes, count, left, right, total):
    def step(at, _):
        for u in range(UNROLL):
            code = codes[at * UNROLL + u]
            b = right[(code >> 10) & 1023]
            out = jnp.dot(left[code & 1023], jnp.concatenate([b, b], axis=0), preferred_element_type=jnp.float32)
            total[code >> 20] += out[:, :128] + out[:, 128:]
        return 0

    lax.fori_loop(0, (count + UNROLL - 1) // UNROLL, step, 0)


def zero_blocks(ref, count):
    def step(b, _):
        ref[b] = jnp.zeros(ref.shape[1:], ref.dtype)
        return 0

    lax.fori_loop(0, count, step, 0)


DEPTH, CHUNK = 3, 20


def chunks(pieces):
    result, at = [], 0
    for piece in pieces:
        parts = -(-piece.shape[0] // CHUNK)
        size = piece.shape[0] // parts
        for part in range(parts):
            result.append((piece, part * size, size, at))
            at += size
    return result


def load_and_split(pieces, stage, sems, blocks, base, prepare=lambda: None):
    copies, parts = [], chunks(pieces)
    for n, (piece, start, size, _) in enumerate(parts):
        slot = stage.at[pl.ds(n % DEPTH * CHUNK, size)]
        copies.append(pltpu.make_async_copy(piece.at[pl.ds(start, size)], slot, sems.at[n]))
    for copy in copies[:DEPTH]:
        copy.start()
    prepare()
    for n, (_, _, size, at) in enumerate(parts):
        copies[n].wait()
        split_blocks(stage, n % DEPTH * CHUNK, blocks, base + at, size)
        if n + DEPTH < len(parts):
            copies[n + DEPTH].start()


def first_kernel(*refs):
    pieces, (blocks, square, stage, sems) = refs[:-4], refs[-4:]

    def prepare():
        blocks[ZERO] = jnp.zeros(blocks.shape[1:], blocks.dtype)
        zero_blocks(square, SPOT + 1)

    load_and_split(pieces, stage, sems, blocks, 0, prepare)


def rows_kernel(_, *refs):
    pieces, (blocks, stage, sems) = refs[:-3], refs[-3:]
    load_and_split(pieces, stage, sems, blocks, OWN)


def early_kernel(codes, cube_codes, counts, _, square_in, *refs):
    pieces, (blocks, square, halves, cube, stage, sems) = refs[:-6], refs[-6:]

    def prepare():
        zero_blocks(cube, CELLS * HALF + 1)
        halves[2 * SPOT] = jnp.zeros(blocks.shape[1:], blocks.dtype)

    load_and_split(pieces, stage, sems, blocks, OWN + ROWS_PART, prepare)
    run_list(codes, counts[0], blocks, blocks, square)
    split_blocks(square, 0, halves, SPOT, SPOT)
    run_list(cube_codes, counts[2], halves, blocks, cube)
    base = counts[7]

    def combine(i, _):
        for f in range(HALF):
            cube[i * HALF + f] = cube[i * HALF + f] - 1.5 * square[i * SLOTS + base + f]
        return 0

    lax.fori_loop(0, CELLS, combine, 0)
    zero_blocks(square, SPOT + 1)


def corner_kernel(_, *refs):
    pieces, (blocks, stage, sems) = refs[:-3], refs[-3:]
    load_and_split(pieces, stage, sems, blocks, EARLY)


def late_kernel(codes, tail_codes, touched, counts, blocks_in, square_in, halves_in, cube_in, *refs):
    pieces, (out, blocks, square, halves, cube, stage, sems) = refs[:-7], refs[-7:]
    load_and_split(pieces, stage, sems, blocks, EARLY + LATE)
    run_list(codes, counts[1], blocks, blocks, square)

    def resplit(n, _):
        o = touched[n]
        high, low = split(square[o])
        halves[o, :, :128] = high
        halves[o, :, 128:] = low
        return 0

    lax.fori_loop(0, counts[6], resplit, 0)
    run_list(tail_codes, counts[3], halves, blocks, cube)
    base = counts[7]
    copies = []
    for i in range(CELLS):
        for f in range(HALF):
            o = i * HALF + f
            stage[o] = 3.0 * square[i * SLOTS + base + f] - 2.0 * cube[o]
        at = pl.ds(i * HALF, HALF)
        copies.append(pltpu.make_async_copy(stage.at[at], out.at[at], sems.at[i]))
        copies[-1].start()
    for copy in copies:
        copy.wait()


def pack_kernel(plan, count, *refs):
    sources, dests, sems = refs[:count], refs[count:-1], refs[-1]
    run_plan(plan, sources, dests, sems)


def pack_far_kernel(plan, source, *refs):
    dests, held, sems = refs[:-2], refs[-2], refs[-1]
    copy = pltpu.make_async_copy(source, held, sems.at[0])
    copy.start()
    copy.wait()
    run_plan(plan, [held], dests, sems)


def run_plan(plan, sources, dests, sems):
    copies = []
    rep = lax.axis_index("rep")
    for n, (d, at, q, start, length) in enumerate(plan):
        if isinstance(start, tuple):
            start = jnp.where(rep == 0, start[0], start[1])
        copies.append(pltpu.make_async_copy(sources[q].at[pl.ds(start, length)], dests[d].at[pl.ds(at, length)], sems.at[n]))
        copies[-1].start()
    for copy in copies:
        copy.wait()


def pack(arrays, wanted, far=False):
    plan, sizes = [], []
    for d, ranges in enumerate(wanted):
        at = 0
        for q, start, length in ranges:
            plan.append((d, at, q, start, length))
            at += length
        sizes.append(at)
    out = pltpu.HBM if far else jax.ShapeDtypeStruct
    held = [pltpu.VMEM(arrays[0].shape, jnp.float32)] if far else []
    kernel = functools.partial(pack_far_kernel, tuple(plan)) if far else functools.partial(pack_kernel, tuple(plan), len(arrays))
    return pl.pallas_call(
        kernel,
        out_shape=[out((n, 128, 128), jnp.float32) for n in sizes],
        in_specs=[anyspace()] * len(arrays),
        out_specs=[hbm() if far else vmem()] * len(sizes),
        scratch_shapes=held + [pltpu.SemaphoreType.DMA((len(plan),))],
        compiler_params=pltpu.CompilerParams(vmem_limit_bytes=3 << 20),
        cost_estimate=pl.CostEstimate(flops=1000, bytes_accessed=1000, transcendentals=0),
        name="pack",
    )(*arrays)


def smem():
    return pl.BlockSpec(memory_space=pltpu.SMEM)


def anyspace():
    return pl.BlockSpec(memory_space=pl.ANY)


def vmem():
    return pl.BlockSpec(memory_space=pltpu.VMEM)


def hbm():
    return pl.BlockSpec(memory_space=pltpu.HBM)


BLOCKS = pltpu.VMEM((TOTAL, 128, 256), jnp.bfloat16)
SQUARE = pltpu.VMEM((SPOT + 1, 128, 128), jnp.float32)
HALVES = pltpu.VMEM((2 * SPOT + 1, 128, 256), jnp.bfloat16)
CUBE = pltpu.VMEM((CELLS * HALF + 1, 128, 128), jnp.float32)


def call(kernel, name, lists, held, pieces, outs, aliases):
    kinds = [hbm() if isinstance(o, jax.ShapeDtypeStruct) else vmem() for o in outs]
    return pl.pallas_call(
        kernel,
        out_shape=outs,
        in_specs=[smem()] * len(lists) + [vmem()] * len(held) + [anyspace()] * len(pieces),
        out_specs=kinds,
        scratch_shapes=[pltpu.VMEM((DEPTH * CHUNK, 128, 128), jnp.float32), pltpu.SemaphoreType.DMA((16,))],
        input_output_aliases={len(lists) + i: o for i, o in aliases.items()},
        compiler_params=pltpu.CompilerParams(vmem_limit_bytes=4 << 20),
        cost_estimate=pl.CostEstimate(flops=1000, bytes_accessed=1000, transcendentals=0),
        name=name,
    )(*lists, *held, *pieces)


def stored_places():
    return jnp.where(lax.axis_index("rep") == 0, block_places(0), block_places(1))


def flat(x):
    return x.reshape(-1, 128, 128)


def body(density, pattern, filt):
    blocks = flat(density)
    row = COLS * HALF
    above, below = shift(pattern, "dom", 1), shift(pattern, "dom", -1)
    own_other = shift(blocks, "rep", 1)
    one, two = pack([blocks], [[(0, (row, 0), 2 * row)], [(0, (0, row), 2 * row)]], far=True)
    above, below, one = lax.optimization_barrier((above, below, one))
    one = cross(one, 1)
    near = jnp.concatenate([above[ROWS - 2:], pattern, below[:2]], axis=0)
    before, after = shift(near[:, 1:], "col", 1), shift(near[:, :1], "col", -1)
    edge_r, edge_l = pack([blocks], [[(0, r * row + q, HALF) for r in range(ROWS)] for q in (HALF, 0)])
    before, after, two, edge_r, edge_l = lax.optimization_barrier((before, after, two, edge_r, edge_l))
    two = cross(two, -1)
    right, left = shift(edge_r, "col", 1), shift(edge_l, "col", -1)
    rim = jnp.concatenate([before, near, after], axis=1)
    own_filt = jnp.pad(filt, ((0, 0), (0, RIM_C - COLS), (0, 0)), constant_values=-1)
    known = lax.all_gather(jnp.concatenate([rim, own_filt], axis=0), "rep", axis=2, tiled=True)
    early_codes, late_codes, cube_codes, tail_codes, touched, counts = make_lists(known, stored_places())
    counts, own_other = lax.optimization_barrier((counts, own_other))
    held, square = call(first_kernel, "first", [], [], [blocks, own_other], [BLOCKS, SQUARE], {})
    held, square, one = lax.optimization_barrier((held, square, one))
    to_r, to_l = pack([one], [[(0, q, HALF), (0, row + q, HALF)] for q in (HALF, 0)])
    corner_r, corner_l = shift(to_r, "col", 1), shift(to_l, "col", -1)
    right, left, to_r, to_l = lax.optimization_barrier((right, left, to_r, to_l))
    (corner,) = pack([right, left], [[(q, (0, HALF), 2 * HALF) for q in (0, 1)]])
    right, left, two, corner = lax.optimization_barrier((right, left, two, corner))
    corner = cross(corner, -1)
    mine = [right, left, one, two]
    others = [shift(p, "rep", 1) for p in mine]
    (held,) = call(rows_kernel, "rows", [], [held], mine, [BLOCKS], {0: 0})
    held, square, halves, cube = call(
        early_kernel, "early", [early_codes, cube_codes, counts], [held, square], others,
        [BLOCKS, SQUARE, HALVES, CUBE], {0: 0, 1: 1},
    )
    held, square, halves, cube, *corners = lax.optimization_barrier(
        (held, square, halves, cube, corner_r, corner_l, corner)
    )
    others = [shift(p, "rep", 1) for p in corners]
    (held,) = call(corner_kernel, "corner", [], [held], corners, [BLOCKS], {0: 0})
    out = jax.ShapeDtypeStruct((CELLS * HALF, 128, 128), jnp.float32)
    out = call(
        late_kernel, "late", [late_codes, tail_codes, touched, counts], [held, square, halves, cube], others,
        [out, BLOCKS, SQUARE, HALVES, CUBE], {0: 1, 1: 2, 2: 3, 3: 4},
    )[0]
    return out.reshape(density.shape)


def solution(mesh):
    in_specs = (P("dom", "col", "rep", None, None), P("dom", "col", "rep"), P("dom", "col", "rep"))
    out_specs = P("dom", "col", "rep", None, None)
    return jax.shard_map(body, mesh=mesh, in_specs=in_specs, out_specs=out_specs, check_vma=False)
```

```python
import functools

import jax
import jax.numpy as jnp
import numpy as np
from jax import lax
from jax.experimental import pallas as pl
from jax.experimental.pallas import tpu as pltpu
from jax.sharding import PartitionSpec as P

UNROLL = 32
ROWS, COLS = 3, 2
HALF = 5
RIM_D, RIM_C = ROWS + 4, COLS + 2
RIM = RIM_D * RIM_C
CELLS = ROWS * COLS
SLOTS = 2 * HALF
OWN = 60
EARLY = 200
ROWS_PART = 70
LATE = 40
ZERO = EARLY + 2 * LATE
TOTAL = ZERO + 1
SPOT = OWN


def block_places(core):
    places = np.zeros((RIM_D, RIM_C, SLOTS), np.int32)
    for rd in range(RIM_D):
        for rc in range(RIM_C):
            for t in range(SLOTS):
                half, s = divmod(t, HALF)
                other = int(half != core)
                mid_d, mid_c = 2 <= rd < 2 + ROWS, 1 <= rc < 1 + COLS
                low, far = int(rd >= 2 + ROWS), int(rc == RIM_C - 1)
                row = rd - 2 - ROWS if low else rd
                if mid_d and mid_c:
                    at = other * 30 + ((rd - 2) * 2 + rc - 1) * 5 + s
                elif mid_d:
                    at = OWN + other * ROWS_PART + far * 15 + (rd - 2) * 5 + s
                elif mid_c:
                    at = OWN + other * ROWS_PART + 30 + int(low != half) * 20 + (row * 2 + rc - 1) * 5 + s
                else:
                    at = EARLY + other * LATE + int(low != half) * 20 + far * 10 + row * 5 + s
                places[rd, rc, t] = at
    return places


def shift(array, axis, step):
    peers = lax.axis_size(axis)
    return lax.ppermute(array, axis, [(i, (i + step) % peers) for i in range(peers)])


def cross(array, step):
    peers = lax.axis_size("dom")
    pairs = [(2 * i + core, (i + (step, -step)[core]) % peers * 2 + core) for i in range(peers) for core in range(2)]
    return lax.ppermute(array, ("dom", "rep"), pairs)


SQUARE_LEN = SPOT * SLOTS + UNROLL
CUBE_LEN = CELLS * HALF * SLOTS + UNROLL
TAIL_LEN = 2 * CELLS * HALF * SLOTS + UNROLL
LANES = 128
NONE = RIM + 3
TABLE = 32


def list_kernel(
    grid, known, stored, early, late, cube, tail, touched, counts, table_v, place_v, table, place, flag, sems
):
    grid_d, grid_c = grid
    dom, col, rep = lax.axis_index("dom"), lax.axis_index("col"), lax.axis_index("rep")
    lane = lax.broadcasted_iota(jnp.int32, (1, LANES), 1)
    names = jnp.full((1, LANES), -5, jnp.int32)
    name = []
    for j in range(RIM):
        d, c = dom * ROWS + (j // RIM_C - 2), col * COLS + (j % RIM_C - 1)
        d = jnp.where(d < 0, d + grid_d, jnp.where(d >= grid_d, d - grid_d, d))
        c = jnp.where(c < 0, c + grid_c, jnp.where(c >= grid_c, c - grid_c, c))
        name.append(d * grid_c + c)
        names = jnp.where(lane == j, name[j], names)
    table_v[...] = jnp.full((TABLE, LANES), -1, jnp.int32)
    for r in range(RIM_D):
        x, at = known[r], stored[r]
        row = jnp.full((RIM_C, LANES), -1, jnp.int32)
        for t in range(SLOTS):
            row = jnp.where(x[:, t:t + 1] == names, at[:, t:t + 1], row)
        table_v[r * RIM_C:(r + 1) * RIM_C, :] = row
    one = pltpu.make_async_copy(table_v, table, sems.at[0])
    one.start()
    for q in range(2):
        for r in range(ROWS):
            x = known[2 + r, 1:1 + COLS] if q == 0 else known[RIM_D + r, :COLS]
            at = jnp.full((COLS, SLOTS), NONE, jnp.int32)
            for j in range(RIM):
                at = jnp.where(x == name[j], j, at)
            place_v[q * CELLS + r * COLS:q * CELLS + (r + 1) * COLS, :SLOTS] = at
    two = pltpu.make_async_copy(place_v, place, sems.at[1])
    two.start()
    two.wait()
    one.wait()

    blank = ZERO | (ZERO << 10) | (SPOT << 20)
    blank_cube = 2 * SPOT | (ZERO << 10) | ((CELLS * HALF) << 20)

    def square_cell(i, carry):
        rows = [place[i, s] for s in range(SLOTS)]
        own = [i * HALF + s % HALF + jnp.where(rep == s // HALF, 0, CELLS * HALF) for s in range(SLOTS)]

        def square_row(f, carry):
            ne, nl, nt = carry
            before = nl
            k = place[CELLS + i, f]
            spot = i * SLOTS + f
            o = spot << 20
            values = [table[j, k] for j in rows]
            for s in range(SLOTS):
                v = values[s]
                code = (own[s] | o) + (v << 10)
                early[ne] = code
                late[nl] = code
                is_late = jnp.where(v >= EARLY, 1, 0)
                ne = ne + jnp.where(v >= 0, 1, 0) - is_late
                nl = nl + is_late
            again = jnp.where(nl > before, 1, 0)
            flag[spot] = again
            touched[nt] = spot
            return ne, nl, nt + again

        return lax.fori_loop(0, SLOTS, square_row, carry)

    def cube_cell(i, carry):
        rows = [place[CELLS + i, g] for g in range(SLOTS)]
        again = [flag[i * SLOTS + g] for g in range(SLOTS)]

        def cube_row(f, carry):
            nc, nt = carry
            k = place[CELLS + i, rep * HALF + f]
            o = (i * SLOTS) | ((i * HALF + f) << 20)
            values = [table[j, k] for j in rows]
            for g in range(SLOTS):
                v = values[g]
                code = (o + (g + SPOT)) | (v << 10)
                hit, is_late = jnp.where(v >= 0, 1, 0), jnp.where(v >= EARLY, 1, 0)
                cube[nc] = code
                nc = nc + hit - is_late
                tail[nt] = code
                nt = nt + is_late
                tail[nt] = code - SPOT
                nt = nt + hit * again[g]
            return nc, nt

        return lax.fori_loop(0, HALF, cube_row, carry)

    zero = jnp.int32(0)
    ne, nl, touches = lax.fori_loop(0, CELLS, square_cell, (zero,) * 3)
    nc, nt = lax.fori_loop(0, CELLS, cube_cell, (zero, zero))
    for u in range(UNROLL):
        early[ne + u] = blank
        late[nl + u] = blank
        cube[nc + u] = blank_cube
        tail[nt + u] = blank_cube
    for q, n in enumerate((ne, nl, nc, nt)):
        counts[q] = n
    counts[6] = touches
    counts[7] = rep * HALF


def make_lists(known, stored):
    grid = (ROWS * lax.axis_size("dom"), COLS * lax.axis_size("col"))
    lengths = (SQUARE_LEN,) * 2 + (CUBE_LEN, TAIL_LEN, SPOT + 1, 8)
    return pl.pallas_call(
        functools.partial(list_kernel, grid),
        out_shape=[jax.ShapeDtypeStruct((n,), jnp.int32) for n in lengths],
        in_specs=[vmem()] * 2,
        out_specs=[smem()] * len(lengths),
        scratch_shapes=[
            pltpu.VMEM((TABLE, LANES), jnp.int32),
            pltpu.VMEM((16, LANES), jnp.int32),
            pltpu.SMEM((TABLE, LANES), jnp.int32),
            pltpu.SMEM((16, LANES), jnp.int32),
            pltpu.SMEM((SPOT,), jnp.int32),
            pltpu.SemaphoreType.DMA((2,)),
        ],
        compiler_params=pltpu.CompilerParams(vmem_limit_bytes=2 << 20),
        cost_estimate=pl.CostEstimate(flops=1000, bytes_accessed=1000, transcendentals=0),
        name="lists",
    )(known, stored)


def split(x):
    high = x.astype(jnp.bfloat16)
    low = (x - high.astype(jnp.float32)).astype(jnp.bfloat16)
    return high, low


def split_blocks(src, src_at, dst, dst_at, count):
    def step(b, _):
        high, low = split(src[src_at + b])
        dst[dst_at + b, :, :128] = high
        dst[dst_at + b, :, 128:] = low
        return 0

    lax.fori_loop(0, count, step, 0, unroll=2)


def run_list(codes, count, left, right, total, unroll=UNROLL):
    def step(at, _):
        for u in range(unroll):
            code = codes[at * unroll + u]
            b = right[(code >> 10) & 1023]
            out = jnp.dot(left[code & 1023], jnp.concatenate([b, b], axis=0), preferred_element_type=jnp.float32)
            total[code >> 20] += out[:, :128] + out[:, 128:]
        return 0

    lax.fori_loop(0, (count + unroll - 1) // unroll, step, 0)


def zero_blocks(ref, count):
    def step(b, _):
        ref[b] = jnp.zeros(ref.shape[1:], ref.dtype)
        return 0

    lax.fori_loop(0, count, step, 0)


DEPTH, CHUNK = 3, 20


def chunks(pieces):
    result, at = [], 0
    for piece in pieces:
        parts = -(-piece.shape[0] // CHUNK)
        size = piece.shape[0] // parts
        for part in range(parts):
            result.append((piece, part * size, size, at))
            at += size
    return result


def load_and_split(pieces, stage, sems, blocks, base, prepare=lambda: None):
    copies, parts = [], chunks(pieces)
    for n, (piece, start, size, _) in enumerate(parts):
        slot = stage.at[pl.ds(n % DEPTH * CHUNK, size)]
        copies.append(pltpu.make_async_copy(piece.at[pl.ds(start, size)], slot, sems.at[n]))
    for copy in copies[:DEPTH]:
        copy.start()
    prepare()
    for n, (_, _, size, at) in enumerate(parts):
        copies[n].wait()
        split_blocks(stage, n % DEPTH * CHUNK, blocks, base + at, size)
        if n + DEPTH < len(parts):
            copies[n + DEPTH].start()


def first_kernel(*refs):
    pieces, (blocks, square, stage, sems) = refs[:-4], refs[-4:]

    def prepare():
        blocks[ZERO] = jnp.zeros(blocks.shape[1:], blocks.dtype)
        zero_blocks(square, SPOT + 1)

    load_and_split(pieces, stage, sems, blocks, 0, prepare)


def rows_kernel(_, *refs):
    pieces, (blocks, stage, sems) = refs[:-3], refs[-3:]
    load_and_split(pieces, stage, sems, blocks, OWN)


def early_kernel(codes, cube_codes, counts, _, square_in, *refs):
    pieces, (blocks, square, halves, cube, stage, sems) = refs[:-6], refs[-6:]

    def prepare():
        zero_blocks(cube, CELLS * HALF + 1)
        halves[2 * SPOT] = jnp.zeros(blocks.shape[1:], blocks.dtype)

    load_and_split(pieces, stage, sems, blocks, OWN + ROWS_PART, prepare)
    run_list(codes, counts[0], blocks, blocks, square)
    split_blocks(square, 0, halves, SPOT, SPOT)
    run_list(cube_codes, counts[2], halves, blocks, cube)
    base = counts[7]

    def combine(i, _):
        for f in range(HALF):
            cube[i * HALF + f] = cube[i * HALF + f] - 1.5 * square[i * SLOTS + base + f]
        return 0

    lax.fori_loop(0, CELLS, combine, 0)
    zero_blocks(square, SPOT + 1)


def corner_kernel(_, *refs):
    pieces, (blocks, stage, sems) = refs[:-3], refs[-3:]
    load_and_split(pieces, stage, sems, blocks, EARLY)


def late_kernel(codes, tail_codes, touched, counts, blocks_in, square_in, halves_in, cube_in, *refs):
    pieces, (out, blocks, square, halves, cube, stage, sems) = refs[:-7], refs[-7:]
    load_and_split(pieces, stage, sems, blocks, EARLY + LATE)
    run_list(codes, counts[1], blocks, blocks, square, 8)

    def resplit(n, _):
        o = touched[n]
        high, low = split(square[o])
        halves[o, :, :128] = high
        halves[o, :, 128:] = low
        return 0

    lax.fori_loop(0, counts[6], resplit, 0)
    run_list(tail_codes, counts[3], halves, blocks, cube, 16)
    base = counts[7]
    copies = []
    for i in range(CELLS):
        for f in range(HALF):
            o = i * HALF + f
            stage[o] = 3.0 * square[i * SLOTS + base + f] - 2.0 * cube[o]
        at = pl.ds(i * HALF, HALF)
        copies.append(pltpu.make_async_copy(stage.at[at], out.at[at], sems.at[i]))
        copies[-1].start()
    for copy in copies:
        copy.wait()


def pack_kernel(plan, count, *refs):
    sources, dests, sems = refs[:count], refs[count:-1], refs[-1]
    run_plan(plan, sources, dests, sems)


def pack_far_kernel(plan, source, *refs):
    dests, held, sems = refs[:-2], refs[-2], refs[-1]
    copy = pltpu.make_async_copy(source, held, sems.at[0])
    copy.start()
    copy.wait()
    run_plan(plan, [held], dests, sems)


def run_plan(plan, sources, dests, sems):
    copies = []
    rep = lax.axis_index("rep")
    for n, (d, at, q, start, length) in enumerate(plan):
        if isinstance(start, tuple):
            start = jnp.where(rep == 0, start[0], start[1])
        copies.append(pltpu.make_async_copy(sources[q].at[pl.ds(start, length)], dests[d].at[pl.ds(at, length)], sems.at[n]))
        copies[-1].start()
    for copy in copies:
        copy.wait()


def pack(arrays, wanted, far=False):
    plan, sizes = [], []
    for d, ranges in enumerate(wanted):
        at = 0
        for q, start, length in ranges:
            plan.append((d, at, q, start, length))
            at += length
        sizes.append(at)
    out = pltpu.HBM if far else jax.ShapeDtypeStruct
    held = [pltpu.VMEM(arrays[0].shape, jnp.float32)] if far else []
    kernel = functools.partial(pack_far_kernel, tuple(plan)) if far else functools.partial(pack_kernel, tuple(plan), len(arrays))
    return pl.pallas_call(
        kernel,
        out_shape=[out((n, 128, 128), jnp.float32) for n in sizes],
        in_specs=[anyspace()] * len(arrays),
        out_specs=[hbm() if far else vmem()] * len(sizes),
        scratch_shapes=held + [pltpu.SemaphoreType.DMA((len(plan),))],
        compiler_params=pltpu.CompilerParams(vmem_limit_bytes=3 << 20),
        cost_estimate=pl.CostEstimate(flops=1000, bytes_accessed=1000, transcendentals=0),
        name="pack",
    )(*arrays)


def smem():
    return pl.BlockSpec(memory_space=pltpu.SMEM)


def anyspace():
    return pl.BlockSpec(memory_space=pl.ANY)


def vmem():
    return pl.BlockSpec(memory_space=pltpu.VMEM)


def hbm():
    return pl.BlockSpec(memory_space=pltpu.HBM)


BLOCKS = pltpu.VMEM((TOTAL, 128, 256), jnp.bfloat16)
SQUARE = pltpu.VMEM((SPOT + 1, 128, 128), jnp.float32)
HALVES = pltpu.VMEM((2 * SPOT + 1, 128, 256), jnp.bfloat16)
CUBE = pltpu.VMEM((CELLS * HALF + 1, 128, 128), jnp.float32)


def call(kernel, name, lists, held, pieces, outs, aliases):
    kinds = [hbm() if isinstance(o, jax.ShapeDtypeStruct) else vmem() for o in outs]
    return pl.pallas_call(
        kernel,
        out_shape=outs,
        in_specs=[smem()] * len(lists) + [vmem()] * len(held) + [anyspace()] * len(pieces),
        out_specs=kinds,
        scratch_shapes=[pltpu.VMEM((DEPTH * CHUNK, 128, 128), jnp.float32), pltpu.SemaphoreType.DMA((16,))],
        input_output_aliases={len(lists) + i: o for i, o in aliases.items()},
        compiler_params=pltpu.CompilerParams(vmem_limit_bytes=4 << 20),
        cost_estimate=pl.CostEstimate(flops=1000, bytes_accessed=1000, transcendentals=0),
        name=name,
    )(*lists, *held, *pieces)


def stored_places():
    return jnp.where(lax.axis_index("rep") == 0, block_places(0), block_places(1))


def flat(x):
    return x.reshape(-1, 128, 128)


def body(density, pattern, filt):
    blocks = flat(density)
    row = COLS * HALF
    above, below = shift(pattern, "dom", 1), shift(pattern, "dom", -1)
    own_other = shift(blocks, "rep", 1)
    one, two = pack([blocks], [[(0, (row, 0), 2 * row)], [(0, (0, row), 2 * row)]], far=True)
    above, below, one = lax.optimization_barrier((above, below, one))
    one = cross(one, 1)
    near = jnp.concatenate([above[ROWS - 2:], pattern, below[:2]], axis=0)
    before, after = shift(near[:, 1:], "col", 1), shift(near[:, :1], "col", -1)
    edge_r, edge_l = pack([blocks], [[(0, r * row + q, HALF) for r in range(ROWS)] for q in (HALF, 0)])
    before, after, two, edge_r, edge_l = lax.optimization_barrier((before, after, two, edge_r, edge_l))
    two = cross(two, -1)
    right, left = shift(edge_r, "col", 1), shift(edge_l, "col", -1)
    rim = jnp.concatenate([before, near, after], axis=1)
    own_filt = jnp.pad(filt, ((0, 0), (0, RIM_C - COLS), (0, 0)), constant_values=-1)
    known = lax.all_gather(jnp.concatenate([rim, own_filt], axis=0), "rep", axis=2, tiled=True)
    early_codes, late_codes, cube_codes, tail_codes, touched, counts = make_lists(known, stored_places())
    counts, own_other = lax.optimization_barrier((counts, own_other))
    held, square = call(first_kernel, "first", [], [], [blocks, own_other], [BLOCKS, SQUARE], {})
    held, square, one = lax.optimization_barrier((held, square, one))
    to_r, to_l = pack([one], [[(0, q, HALF), (0, row + q, HALF)] for q in (HALF, 0)])
    corner_r, corner_l = shift(to_r, "col", 1), shift(to_l, "col", -1)
    right, left, to_r, to_l = lax.optimization_barrier((right, left, to_r, to_l))
    (corner,) = pack([right, left], [[(q, (0, HALF), 2 * HALF) for q in (0, 1)]])
    right, left, two, corner = lax.optimization_barrier((right, left, two, corner))
    corner = cross(corner, -1)
    mine = [right, left, one, two]
    others = [shift(p, "rep", 1) for p in mine]
    (held,) = call(rows_kernel, "rows", [], [held], mine, [BLOCKS], {0: 0})
    held, square, halves, cube = call(
        early_kernel, "early", [early_codes, cube_codes, counts], [held, square], others,
        [BLOCKS, SQUARE, HALVES, CUBE], {0: 0, 1: 1},
    )
    held, square, halves, cube, *corners = lax.optimization_barrier(
        (held, square, halves, cube, corner_r, corner_l, corner)
    )
    others = [shift(p, "rep", 1) for p in corners]
    (held,) = call(corner_kernel, "corner", [], [held], corners, [BLOCKS], {0: 0})
    out = jax.ShapeDtypeStruct((CELLS * HALF, 128, 128), jnp.float32)
    out = call(
        late_kernel, "late", [late_codes, tail_codes, touched, counts], [held, square, halves, cube], others,
        [out, BLOCKS, SQUARE, HALVES, CUBE], {0: 1, 1: 2, 2: 3, 3: 4},
    )[0]
    return out.reshape(density.shape)


def solution(mesh):
    in_specs = (P("dom", "col", "rep", None, None), P("dom", "col", "rep"), P("dom", "col", "rep"))
    out_specs = P("dom", "col", "rep", None, None)
    return jax.shard_map(body, mesh=mesh, in_specs=in_specs, out_specs=out_specs, check_vma=False)
```
